128 devices in a mesh: row: 16 (over y_lo, z, core), col: 8 (over x, y_hi).
Axes of the slice: x: 4, y: 4 (y_hi: 2, y_lo: 2; y = y_hi * 2 + y_lo), z: 4, core: 2. Of those that a mesh axis runs over, the one named last changes fastest.
Arguments:
- iterate: float32 [3072, 8192], P(('row', 'col')), may hold values from -0.030835584 to 0.030835584
Outputs:
- update: float32 [3072, 8192], P(('row', 'col'))
The draws below stay inside these ranges and needn't reach their ends.
All inputs are finite; a program needn't handle non-finite values.
Results may differ from the reference program's by a relative error of at most 0.0003.
Values sent between devices are 32-bit elements; how exact they have to be, the bound alone decides.
A program may use at most 64 MiB of HBM per device.

```python
import math
import jax
import jax.numpy as jnp
from jax import lax

ROWS = 3072
COLS = 8192


def draw_iterate(key, part):
    key = jax.random.fold_in(key, 5)
    spread = 0.9 / (COLS ** 0.5 + ROWS ** 0.5)
    values = jax.random.truncated_normal(key, -5.0, 5.0, (ROWS, COLS), jnp.float32)
    return (values * spread).astype(jnp.float32)


def setup_inputs(seed: int = 0) -> dict:
    streams_of = jax.random.split(jax.random.key(seed), 2)
    iterate = draw_iterate(jax.random.fold_in(streams_of[1], 71), 0)
    return dict(iterate=iterate)


def reference(iterate):
    highest = lax.Precision.HIGHEST
    gram = jnp.dot(iterate, iterate.T, precision=highest, preferred_element_type=jnp.float32)
    once_applied = jnp.dot(gram, iterate, precision=highest, preferred_element_type=jnp.float32)
    twice_applied = jnp.dot(gram, once_applied, precision=highest, preferred_element_type=jnp.float32)
    factor = 0.2 * math.sqrt(max(ROWS, COLS))
    polished = 3.4445 * iterate - 4.775 * once_applied + 2.0315 * twice_applied
    return (factor * polished).astype(jnp.float32)
```

```python
import functools
import math

import jax
import jax.numpy as jnp
from jax import lax
from jax.experimental import pallas as pl
from jax.experimental.pallas import tpu as pltpu
from jax.sharding import Mesh, PartitionSpec as P

AXES = ("y_lo", "z", "core", "x", "y_hi")
SIDE = 4
BANDS = 8
PIECE = 24
BAND = SIDE * SIDE * PIECE
ROWS = BANDS * BAND
WIDTH = 512
COLS = SIDE * SIDE * WIDTH
FACTOR = 0.2 * math.sqrt(max(ROWS, COLS))
F32, BF16 = jnp.float32, jnp.bfloat16
MESH = pl.DeviceIdType.MESH
N_SEMS = 200


def halves(value):
    high = value.astype(BF16)
    return high, (value - high.astype(F32)).astype(BF16)


def kernel(x_ref, o_ref, X, Xh, Xl, Gp, R1, R2, S1, R3, G, Gh, Gl, O, Oh, Ol, T, ss, rs):
    x, z, core = lax.axis_index("x"), lax.axis_index("z"), lax.axis_index("core")
    y = lax.axis_index("y_hi") * 2 + lax.axis_index("y_lo")
    v = jnp.where(core == 0, y, x)
    u = jnp.where(core == 0, x, y)

    def wrap(i):
        return lax.rem(i + 4, 4)

    def place(dv=0, du=0):
        vv, uu = wrap(v + dv), wrap(u + du)
        return jnp.where(core == 0, uu, vv), jnp.where(core == 0, vv, uu)

    def device(dv=0, du=0, dz=0, other=False):
        px, py = place(dv, du)
        return {
            "x": px,
            "y_hi": py // 2,
            "y_lo": lax.rem(py, 2),
            "z": wrap(z + dz),
            "core": 1 - core if other else core,
        }

    def columns(px, py):
        return pl.ds(pl.multiple_of((px * 4 + py) * WIDTH, WIDTH), WIDTH)

    count = [0]
    started = []

    def send(src, dst, **to):
        i = count[0]
        count[0] += 1
        copy = pltpu.make_async_remote_copy(
            src_ref=src, dst_ref=dst, send_sem=ss.at[i], recv_sem=rs.at[i], device_id=device(**to), device_id_type=MESH
        )
        copy.start()
        started.append(copy)
        return copy

    plane = [(dv, du) for dv in (0, 1, 3, 2) for du in range(4) if dv or du]
    peers = [dict(dv=dv, du=du) for dv, du in plane] + [dict(dz=1), dict(dz=-1), dict(other=True)]
    barrier = pltpu.get_barrier_semaphore()
    for peer in peers:
        pl.semaphore_signal(barrier, inc=1, device_id=device(**peer), device_id_type=MESH)
    pl.semaphore_wait(barrier, len(peers))

    def band(dz=0, other=False):
        return wrap(z + dz) * 2 + (1 - core if other else core)

    mine = band()
    steps = [
        ((v, 0), (v, 1)),
        ((wrap(v - 1), 0), (wrap(v + 1), 1)),
        ((wrap(v - 1), 1), (wrap(v + 1), 0)),
        ((wrap(v + 2), 0), (wrap(v + 2), 1)),
    ]

    class Gather:
        def __init__(self, buf):
            self.buf = buf
            self.up, self.down, self.up2, self.down2 = [], [], [], []
            self.side = {}

        def part(self, b, k, i):
            vv, s = steps[k][i]
            return self.buf.at[b, vv, pl.ds(2 * s, 2)]

        def own(self, k):
            self.up.append([send(self.part(mine, k, i), self.part(mine, k, i), dz=1) for i in (0, 1)])
            down = [send(self.part(mine, k, i), self.part(mine, k, i), dz=-1) for i in (1, 0)]
            self.down.append(down[::-1])

        def relay(self, k):
            below, above = band(-1), band(1)
            self.up[k][0].wait_recv()
            self.up2.append(send(self.part(below, k, 0), self.part(below, k, 0), dz=1))
            self.down[k][1].wait_recv()
            self.down2.append(send(self.part(above, k, 1), self.part(above, k, 1), dz=-1))
            self.up[k][1].wait_recv()
            self.down[k][0].wait_recv()

        def far(self):
            for copy in self.up2 + self.down2:
                copy.wait_recv()

        def across(self, dz):
            b = band(dz)
            self.side[dz] = send(self.buf.at[b], self.buf.at[b], other=True)

    incoming = {}
    for dv, du in plane:
        incoming[dv, du] = send(x_ref.at[:, columns(*place(dv, du))], X.at[mine, v, u], dv=dv, du=du)
    X[mine, v, u] = x_ref[:, columns(x, y)]

    gx = Gather(X)
    for k, groups in enumerate(((0,), (1, 3), (), (2,))):
        for dv in groups:
            for du in range(4):
                if dv or du:
                    incoming[dv, du].wait_recv()
        gx.own(k)
    gx.across(0)

    def rows_of(b):
        return pl.multiple_of(b * BAND, BAND)

    def split(buf, high, low, b):
        def body(i, carry):
            h, l = halves(buf[b, i].reshape(SIDE * PIECE, WIDTH))
            at = pl.ds(pl.multiple_of(b * BAND + i * 96, 96), 96)
            high[at, :] = h
            low[at, :] = l
            return carry

        lax.fori_loop(0, SIDE, body, 0)

    def dot_t(a, b):
        return lax.dot_general(a, b, (((1,), (1,)), ((), ())), preferred_element_type=F32)

    def dot(a, b):
        return jnp.dot(a, b, preferred_element_type=F32)

    def gram(i, b):
        own, at = pl.ds(rows_of(mine), BAND), pl.ds(rows_of(b), BAND)
        ah, al, bh, bl = Xh[own, :], Xl[own, :], Xh[at, :], Xl[at, :]
        Gp[i] = (dot_t(ah, bh) + (dot_t(al, bh) + dot_t(ah, bl))).reshape(4, 4, PIECE, BAND)

    s1, s2, s3, t1 = {}, {}, {}, {}
    vp, vm, v2 = wrap(v + 1), wrap(v - 1), wrap(v + 2)

    def rs1(i):
        s1[i] = (
            send(Gp.at[i, v2, pl.ds(0, 2)], R1.at[i, 0], dv=1),
            send(Gp.at[i, v2, pl.ds(2, 2)], R1.at[i, 1], dv=-1),
        )

    def rs2(i):
        s1[i][0].wait_recv()
        Gp[i, vp, 0:2] += R1[i, 0]
        up = send(Gp.at[i, vp], R2.at[i, 0], dv=1)
        s1[i][1].wait_recv()
        Gp[i, vm, 2:4] += R1[i, 1]
        s2[i] = (up, send(Gp.at[i, vm], R2.at[i, 1], dv=-1))

    def rs3(i):
        for copy in s2[i]:
            copy.wait_recv()
        S1[i] = Gp[i, v] + (R2[i, 0] + R2[i, 1])
        s3[i] = [send(S1.at[i, wrap(u + d)], R3.at[i, d - 1], du=d) for d in (1, 3, 2)]

    def rs4(i, b):
        for copy in s3[i]:
            copy.wait_recv()
        G[v, b, u] = (S1[i, u] + R3[i, 0]) + (R3[i, 1] + R3[i, 2])
        t1[i] = [send(G.at[v, b, u], G.at[v, b, u], du=d) for d in (1, 3, 2)]

    order = [band(), band(0, True), band(-1), band(1), band(-1, True), band(1, True), band(2), band(2, True)]

    split(X, Xh, Xl, order[0])
    gram(0, order[0])
    rs1(0)
    gx.side[0].wait_recv()
    split(X, Xh, Xl, order[1])
    gram(1, order[1])
    rs1(1)
    rs2(0)
    rs2(1)
    gx.relay(0)
    rs3(0)
    rs3(1)
    gx.relay(1)
    rs4(0, order[0])
    rs4(1, order[1])
    gx.relay(2)
    gx.relay(3)
    gx.across(-1)
    gx.across(1)
    for i in (2, 3):
        split(X, Xh, Xl, order[i])
        gram(i, order[i])
        rs1(i)
    for i, dz in ((4, -1), (5, 1)):
        gx.side[dz].wait_recv()
        split(X, Xh, Xl, order[i])
        gram(i, order[i])
        rs1(i)
        rs2(i - 2)
    rs3(2)
    rs2(4)
    rs3(3)
    rs2(5)
    gx.far()
    gx.across(2)
    split(X, Xh, Xl, order[6])
    gram(6, order[6])
    rs1(6)
    gx.side[2].wait_recv()
    split(X, Xh, Xl, order[7])
    gram(7, order[7])
    rs1(7)
    rs3(4)
    rs3(5)
    rs2(6)
    rs2(7)
    for i in (2, 3, 4, 5):
        rs4(i, order[i])
    rs3(6)
    rs3(7)
    rs4(6, order[6])
    rs4(7, order[7])

    for i in range(BANDS):
        for copy in t1[i]:
            copy.wait_recv()

    def gram_part(part):
        return G.at[part[0], :, pl.ds(2 * part[1], 2)]

    def forward(part, dv):
        return send(gram_part(part), gram_part(part), dv=dv)

    up = [forward((v, 0), 1), forward((v, 1), 1)]
    down = [forward((v, 1), -1), forward((v, 0), -1)]

    go = Gather(O)

    def once(k):
        at = []
        for vv, s in steps[k]:
            rows = pl.ds(pl.multiple_of(vv * 96 + s * 48, 16), 48)
            at.append(rows)
            for b in range(BANDS):
                h, l = halves(G[vv, b, pl.ds(2 * s, 2)].reshape(48, BAND))
                Gh[rows, b * BAND : (b + 1) * BAND] = h
                Gl[rows, b * BAND : (b + 1) * BAND] = l
        high = [Gh[rows, :] for rows in at]
        low = [Gl[rows, :] for rows in at]
        first = dot(jnp.concatenate(high + low, axis=0), Xh[...])
        result = first[:96] + (first[96:] + dot(jnp.concatenate(high, axis=0), Xl[...]))
        for i, (vv, s) in enumerate(steps[k]):
            O[mine, vv, pl.ds(2 * s, 2)] = result[48 * i : 48 * (i + 1)].reshape(2, PIECE, WIDTH)
        go.own(k)

    once(0)
    up[0].wait_recv()
    up2 = forward((vm, 0), 1)
    down[0].wait_recv()
    down2 = forward((vp, 1), -1)
    once(1)
    go.relay(0)
    up[1].wait_recv()
    down[1].wait_recv()
    once(2)
    go.relay(1)
    up2.wait_recv()
    down2.wait_recv()
    once(3)
    go.across(0)
    go.relay(2)

    def twice(b, first=False):
        split(O, Oh, Ol, b)
        cols, at = pl.ds(pl.multiple_of(b * BAND, 128), BAND), pl.ds(rows_of(b), BAND)
        gh, gl, oh, ol = Gh[:, cols], Gl[:, cols], Oh[at, :], Ol[at, :]
        term = (dot(gh, oh) + (dot(gl, oh) + dot(gh, ol))).reshape(4, 4, PIECE, WIDTH)
        T[...] = term if first else T[...] + term

    twice(order[0], True)
    go.side[0].wait_recv()
    twice(order[1])
    go.relay(3)
    go.across(-1)
    go.across(1)
    twice(order[2])
    twice(order[3])
    go.far()
    go.across(2)
    for i, dz in ((4, -1), (5, 1)):
        go.side[dz].wait_recv()
        twice(order[i])
    twice(order[6])
    go.side[2].wait_recv()
    twice(order[7])
    T[...] = FACTOR * (3.4445 * X[mine] - 4.775 * O[mine] + 2.0315 * T[...])

    outgoing = []
    for dv, du in plane:
        outgoing.append(
            send(T.at[wrap(v + dv), wrap(u + du)], o_ref.at[:, columns(x, y)], dv=dv, du=du)
        )
    o_ref[:, columns(x, y)] = T[v, u]
    for copy in outgoing:
        copy.wait_recv()
    for copy in started:
        copy.wait_send()


def per_device(iterate):
    vmem = functools.partial(pl.BlockSpec, memory_space=pltpu.VMEM)
    shapes = [
        ((BANDS, 4, 4, PIECE, WIDTH), F32),
        ((ROWS, WIDTH), BF16),
        ((ROWS, WIDTH), BF16),
        ((BANDS, 4, 4, PIECE, BAND), F32),
        ((BANDS, 2, 2, PIECE, BAND), F32),
        ((BANDS, 2, 4, PIECE, BAND), F32),
        ((BANDS, 4, PIECE, BAND), F32),
        ((BANDS, 3, PIECE, BAND), F32),
        ((4, BANDS, 4, PIECE, BAND), F32),
        ((BAND, ROWS), BF16),
        ((BAND, ROWS), BF16),
        ((BANDS, 4, 4, PIECE, WIDTH), F32),
        ((ROWS, WIDTH), BF16),
        ((ROWS, WIDTH), BF16),
        ((4, 4, PIECE, WIDTH), F32),
    ]
    return pl.pallas_call(
        kernel,
        out_shape=jax.ShapeDtypeStruct((PIECE, COLS), F32),
        in_specs=[vmem()],
        out_specs=vmem(),
        scratch_shapes=[pltpu.VMEM(shape, dtype) for shape, dtype in shapes]
        + [pltpu.SemaphoreType.DMA((N_SEMS,)), pltpu.SemaphoreType.DMA((N_SEMS,))],
        compiler_params=pltpu.CompilerParams(
            collective_id=0, has_side_effects=True, vmem_limit_bytes=60 * 1024 * 1024
        ),
        cost_estimate=pl.CostEstimate(
            flops=6 * 3 * BAND * ROWS * WIDTH, bytes_accessed=2 * 4 * PIECE * COLS, transcendentals=0
        ),
    )(iterate)


def solution(mesh):
    fine = Mesh(mesh.devices.reshape(2, 4, 2, 4, 2), AXES)
    spec = P(AXES, None)
    return jax.shard_map(per_device, mesh=fine, in_specs=(spec,), out_specs=spec, check_vma=False)
```

```python
import math

import jax
import jax.numpy as jnp
from jax import lax
from jax.experimental import pallas as pl
from jax.experimental.pallas import tpu as pltpu
from jax.sharding import Mesh, PartitionSpec as P

AXES = ("y_lo", "z", "core", "x", "y_hi")
BANDS = 8
GROUPS = 3
LANES = 128
BAND = GROUPS * LANES
ROWS = BANDS * BAND
WIDTH = 512
COLS = 16 * WIDTH
FACTOR = 0.2 * math.sqrt(max(ROWS, COLS))
F32, BF16 = jnp.float32, jnp.bfloat16
MESH = pl.DeviceIdType.MESH
N_SEMS = 136
UNITS = (3, 3, 4, 4, 4, 2, 2, 2)
FIRST = tuple(sum(UNITS[:c]) for c in range(len(UNITS)))
CHUNK = tuple(slice(LANES * a, LANES * (a + n)) for a, n in zip(FIRST, UNITS))
ORDER = (
    "z0 z1 z2 g0",
    "g1 r0 a0 p0",
    "g2 p1 r1 a1",
    "s0 p2 g3 s1",
    "q0 r2 a2 s2",
    "p3 g4 f0 q1",
    "g5 q2 f1 s3",
    "g6 p4 f2 p5",
    "g7 p6 q3 s4",
    "s5 p7 s6 q4",
    "q5 s7 q6 q7",
)


def halves(value):
    high = value.astype(BF16)
    return high, (value - high.astype(F32)).astype(BF16)


def kernel(x_ref, o_ref, X, Xh, Xl, Gp, R1, R2, S1, R3, G, Gh, Gl, O, Oh, Ol, T, ss, rs):
    x, z, core = lax.axis_index("x"), lax.axis_index("z"), lax.axis_index("core")
    y = lax.axis_index("y_hi") * 2 + lax.axis_index("y_lo")
    v = jnp.where(core == 0, y, x)
    u = jnp.where(core == 0, x, y)

    def wrap(i):
        return lax.rem(i + 4, 4)

    def place(dv=0, du=0):
        vv, uu = wrap(v + dv), wrap(u + du)
        return jnp.where(core == 0, uu, vv), jnp.where(core == 0, vv, uu)

    def device(dv=0, du=0, dz=0, other=False):
        px, py = place(dv, du)
        return {
            "x": px,
            "y_hi": py // 2,
            "y_lo": lax.rem(py, 2),
            "z": wrap(z + dz),
            "core": 1 - core if other else core,
        }

    def columns(px, py):
        return pl.ds(pl.multiple_of((px * 4 + py) * WIDTH, WIDTH), WIDTH)

    count = [0]
    leaving = []

    def fresh(size):
        i = count[0]
        count[0] += 1
        leaving.append((i, size))
        return i

    def send(i, src, dst, **to):
        pltpu.make_async_remote_copy(
            src_ref=src, dst_ref=dst, send_sem=ss.at[i], recv_sem=rs.at[i], device_id=device(**to), device_id_type=MESH
        ).start()

    def send_one(src, dst, **to):
        i = fresh(src)
        send(i, src, dst, **to)
        return i, src

    def arrive(pair):
        i, size = pair
        pltpu.make_async_copy(size, size, rs.at[i]).wait()

    plane = [(dv, du) for dv in (0, 1, 3, 2) for du in range(4) if dv or du]
    peers = [dict(dv=dv, du=du) for dv, du in plane] + [dict(dz=1), dict(dz=-1), dict(other=True)]
    barrier = pltpu.get_barrier_semaphore()
    for peer in peers:
        pl.semaphore_signal(barrier, inc=1, device_id=device(**peer), device_id_type=MESH)
    pl.semaphore_wait(barrier, len(peers))

    def band(dz=0, other=False):
        return wrap(z + dz) * 2 + (1 - core if other else core)

    mine, sibling = band(), band(0, True)
    near = [band(-1), band(1), band(-1, True), band(1, True)]
    away = [band(2), band(2, True)]
    rows = [[(mine, j) for j in range(GROUPS)], [(sibling, j) for j in range(GROUPS)]]
    rows += [[(b, j) for b in near] for j in range(GROUPS)]
    rows += [[(b, j) for b in away] for j in range(GROUPS)]

    i_out = fresh(x_ref.at[:, :, pl.ds(0, 15 * WIDTH)])
    i_in = [i_out, count[0], count[0] + 1]
    count[0] += 2
    for j in range(GROUPS):
        for dv, du in plane:
            pltpu.make_async_remote_copy(
                src_ref=x_ref.at[j, :, columns(*place(dv, du))],
                dst_ref=X.at[mine, j, v, u],
                send_sem=ss.at[i_out],
                recv_sem=rs.at[i_in[j]],
                device_id=device(dv=dv, du=du),
                device_id_type=MESH,
            ).start()
        pltpu.make_async_copy(x_ref.at[j, :, columns(x, y)], X.at[mine, j, v, u], rs.at[i_in[j]]).start()

    def dot_t(a, b):
        return lax.dot_general(a, b, (((1,), (1,)), ((), ())), preferred_element_type=F32)

    def dot(a, b):
        return jnp.dot(a, b, preferred_element_type=F32)

    def split(buf, high, low, c):
        for i, (b, j) in enumerate(rows[c]):
            at = slice((FIRST[c] + i) * LANES, (FIRST[c] + i + 1) * LANES)
            high[at, :], low[at, :] = halves(buf[b, j].reshape(LANES, WIDTH))

    vp, vm, v2 = wrap(v + 1), wrap(v - 1), wrap(v + 2)
    up, down, up2, down2, side = {}, {}, {}, {}, {}
    r1, r2, r3, r4 = {}, {}, {}, {}
    side["own"] = (fresh(X.at[0]), X.at[0])

    def z_step(j):
        part = X.at[mine, j]
        arrive((i_in[j], part))
        up[j] = send_one(part, part, dz=1)
        down[j] = send_one(part, part, dz=-1)
        send(side["own"][0], part, part, other=True)

    def r_step(j):
        arrive(up[j])
        half = X.at[near[0], j, pl.ds(0, 2)]
        up2[j] = send_one(half, half, dz=1)
        arrive(down[j])
        half = X.at[near[1], j, pl.ds(2, 2)]
        down2[j] = send_one(half, half, dz=-1)

    def a_step(j):
        side[j] = (fresh(X.at[0, pl.ds(0, 2)]), X.at[0, pl.ds(0, 2)])
        for b in near[:2]:
            send(side[j][0], X.at[b, j], X.at[b, j], other=True)

    def f_step(j):
        arrive(up2[j])
        arrive(down2[j])
        part = X.at[away[0], j]
        side[GROUPS + j] = send_one(part, part, other=True)

    def g_step(c):
        if c:
            arrive(side["own" if c == 1 else c - 2])
        split(X, Xh, Xl, c)
        at = CHUNK[c]
        ah, al, bh, bl = Xh[:BAND, :], Xl[:BAND, :], Xh[at, :], Xl[at, :]
        term = dot_t(ah, bh) + (dot_t(al, bh) + dot_t(ah, bl))
        Gp[:, :, :, :, at] = term.reshape(GROUPS, 4, 4, 8, LANES * UNITS[c])
        r1[c] = (
            send_one(Gp.at[:, v2, pl.ds(0, 2), :, at], R1.at[0, :, :, :, at], dv=1),
            send_one(Gp.at[:, v2, pl.ds(2, 2), :, at], R1.at[1, :, :, :, at], dv=-1),
        )

    def p_step(c):
        at = CHUNK[c]
        arrive(r1[c][0])
        Gp[:, vp, 0:2, :, at] += R1[0, :, :, :, at]
        first = send_one(Gp.at[:, vp, :, :, at], R2.at[0, :, :, :, at], dv=1)
        arrive(r1[c][1])
        Gp[:, vm, 2:4, :, at] += R1[1, :, :, :, at]
        r2[c] = (first, send_one(Gp.at[:, vm, :, :, at], R2.at[1, :, :, :, at], dv=-1))

    def s_step(c):
        at = CHUNK[c]
        for pair in r2[c]:
            arrive(pair)
        S1[:, :, :, at] = Gp[:, v, :, :, at] + (R2[0, :, :, :, at] + R2[1, :, :, :, at])
        size = R3.at[:, :, :, at]
        r3[c] = (fresh(size), size)
        for d in (1, 3, 2):
            send(r3[c][0], S1.at[:, wrap(u + d), :, at], R3.at[d - 1, :, :, at], du=d)

    def q_step(c):
        at = CHUNK[c]
        arrive(r3[c])
        G[:, v, u, :, at] = (S1[:, u, :, at] + R3[0, :, :, at]) + (R3[1, :, :, at] + R3[2, :, :, at])
        r4[c] = (fresh(r3[c][1]), r3[c][1])
        mine_of = G.at[:, v, u, :, at]
        for d in (1, 3, 2):
            send(r4[c][0], mine_of, mine_of, du=d)

    steps = dict(z=z_step, r=r_step, a=a_step, f=f_step, g=g_step, p=p_step, s=s_step, q=q_step)
    for line in ORDER:
        for step in line.split():
            steps[step[0]](int(step[1:]))
    for c in range(len(UNITS)):
        arrive(r4[c])

    def forward(vv, uu, dv):
        part = G.at[:, vv, uu]
        return send_one(part, part, dv=dv)

    rise = [forward(v, i, 1) for i in range(4)]
    fall = [forward(v, 3 - i, -1) for i in range(4)]
    rise2, fall2 = [], []

    takes = [((v, 0, 2), (v, 2, 2))]
    takes += [((vm, i, 1), (vp, 3 - i, 1)) for i in range(4)]
    takes += [((v2, i, 1), (v2, 3 - i, 1)) for i in range(2)]
    o_up, o_down, o_up2, o_down2 = [], [], [], []
    o_side = {key: (fresh(O.at[0]), O.at[0]) for key in ("own", "low", "high", "far")}

    def part_of(b, take):
        vv, first, n = take
        return O.at[b, :, vv, pl.ds(first, n)]

    def across(key, b, *parts):
        for take in parts:
            send(o_side[key][0], part_of(b, take), part_of(b, take), other=True)

    def once(k):
        at = []
        for vv, first, n in takes[k]:
            for j in range(GROUPS):
                h, l = halves(G[j, vv, pl.ds(first, n)].reshape(8 * n, ROWS))
                at.append((j, vv, first, n, h, l))
        high = jnp.concatenate([part[4] for part in at], axis=0)
        low = jnp.concatenate([part[5] for part in at], axis=0)
        m = high.shape[0]
        first_two = dot(jnp.concatenate([high, low], axis=0), Xh[...])
        result = first_two[:m] + (first_two[m:] + dot(high, Xl[...]))
        row = 0
        for j, vv, first, n, _, _ in at:
            O[mine, j, vv, pl.ds(first, n)] = result[row : row + 8 * n].reshape(n, 8, WIDTH)
            row += 8 * n
        a, b = takes[k]
        size = O.at[0, :, 0, pl.ds(0, 2 * a[2])]
        o_up.append((fresh(size), size))
        o_down.append((fresh(size), size))
        for take in (a, b):
            send(o_up[k][0], part_of(mine, take), part_of(mine, take), dz=1)
        for take in (b, a):
            send(o_down[k][0], part_of(mine, take), part_of(mine, take), dz=-1)
        across("own", mine, a, b)

    def pass_on(k):
        a, b = takes[k]
        arrive(o_up[k])
        o_up2.append(send_one(part_of(near[0], a), part_of(near[0], a), dz=1))
        arrive(o_down[k])
        o_down2.append(send_one(part_of(near[1], b), part_of(near[1], b), dz=-1))
        across("low", near[0], a, b)
        across("high", near[1], a, b)

    def far(k):
        arrive(o_up2[k])
        arrive(o_down2[k])
        across("far", away[0], *takes[k])

    once(0)
    for k in range(1, 7):
        if k < 5:
            arrive(rise[k - 1])
            if k < 3:
                rise2.append(forward(vm, k - 1, 1))
            arrive(fall[k - 1])
            if k < 3:
                fall2.append(forward(vp, 4 - k, -1))
        else:
            arrive(rise2[k - 5])
            arrive(fall2[k - 5])
        once(k)
        if k > 1:
            pass_on(k - 2)
        if k > 3:
            far(k - 4)
    for j in range(GROUPS):
        at = slice(j * LANES, (j + 1) * LANES)
        Gh[at, :], Gl[at, :] = halves(G[j].reshape(LANES, ROWS))

    def twice(c):
        split(O, Oh, Ol, c)
        at = CHUNK[c]
        gh, gl, oh, ol = Gh[:, at], Gl[:, at], Oh[at, :], Ol[at, :]
        term = (dot(gh, oh) + (dot(gl, oh) + dot(gh, ol))).reshape(GROUPS, 4, 4, 8, WIDTH)
        T[...] = T[...] + term if c else term

    twice(0)
    pass_on(5)
    far(3)
    arrive(o_side["own"])
    twice(1)
    pass_on(6)
    far(4)
    arrive(o_side["low"])
    arrive(o_side["high"])
    for c in (2, 3, 4):
        twice(c)
    far(5)
    far(6)
    arrive(o_side["far"])
    for c in (5, 6, 7):
        twice(c)
    T[...] = FACTOR * (3.4445 * X[mine] - 4.775 * O[mine] + 2.0315 * T[...])

    i_out = fresh(o_ref.at[:, :, pl.ds(0, 15 * WIDTH)])
    mine_at = o_ref.at[:, :, columns(x, y)]
    for dv, du in plane:
        send(i_out, T.at[:, wrap(v + dv), wrap(u + du)], mine_at, dv=dv, du=du)
    pltpu.make_async_copy(T.at[:, v, u], mine_at, rs.at[i_out]).start()
    arrive((i_out, o_ref))
    for i, size in leaving:
        pltpu.make_async_copy(size, size, ss.at[i]).wait()
    if count[0] > N_SEMS:
        raise ValueError(count[0])


def per_device(iterate):
    vmem = pl.BlockSpec(memory_space=pltpu.VMEM)
    whole, gram, band = (BANDS, GROUPS, 4, 4, 8, WIDTH), (GROUPS, 4, 4, 8, ROWS), (BAND, ROWS)
    shapes = [
        (whole, F32),
        ((ROWS, WIDTH), BF16),
        ((ROWS, WIDTH), BF16),
        (gram, F32),
        ((2, GROUPS, 2, 8, ROWS), F32),
        ((2, GROUPS, 4, 8, ROWS), F32),
        ((GROUPS, 4, 8, ROWS), F32),
        ((3, GROUPS, 8, ROWS), F32),
        (gram, F32),
        (band, BF16),
        (band, BF16),
        (whole, F32),
        ((ROWS, WIDTH), BF16),
        ((ROWS, WIDTH), BF16),
        ((GROUPS, 4, 4, 8, WIDTH), F32),
    ]
    update = pl.pallas_call(
        kernel,
        out_shape=jax.ShapeDtypeStruct((GROUPS, 8, COLS), F32),
        in_specs=[vmem],
        out_specs=vmem,
        scratch_shapes=[pltpu.VMEM(shape, dtype) for shape, dtype in shapes]
        + [pltpu.SemaphoreType.DMA((N_SEMS,)), pltpu.SemaphoreType.DMA((N_SEMS,))],
        compiler_params=pltpu.CompilerParams(
            collective_id=0, has_side_effects=True, vmem_limit_bytes=50 * 1024 * 1024
        ),
        cost_estimate=pl.CostEstimate(
            flops=6 * 3 * BAND * ROWS * WIDTH, bytes_accessed=2 * 4 * GROUPS * 8 * COLS, transcendentals=0
        ),
    )(iterate.reshape(GROUPS, 8, COLS))
    return update.reshape(GROUPS * 8, COLS)


def solution(mesh):
    fine = Mesh(mesh.devices.reshape(2, 4, 2, 4, 2), AXES)
    spec = P(AXES, None)
    return jax.shard_map(per_device, mesh=fine, in_specs=(spec,), out_specs=spec, check_vma=False)
```

```python
import math

import jax
import jax.numpy as jnp
from jax import lax
from jax.experimental import pallas as pl
from jax.experimental.pallas import tpu as pltpu
from jax.sharding import Mesh, PartitionSpec as P

AXES = ("y_lo", "z", "core", "x", "y_hi")
BANDS = 8
GROUPS = 3
LANES = 128
BAND = GROUPS * LANES
ROWS = BANDS * BAND
WIDTH = 512
COLS = 16 * WIDTH
FACTOR = 0.2 * math.sqrt(max(ROWS, COLS))
F32, BF16 = jnp.float32, jnp.bfloat16
MESH = pl.DeviceIdType.MESH
N_SEMS = 117
UNITS = (3, 3, 4, 4, 4, 2, 2, 2)
FIRST = tuple(sum(UNITS[:c]) for c in range(len(UNITS)))
CHUNK = tuple(slice(LANES * a, LANES * (a + n)) for a, n in zip(FIRST, UNITS))
LAST = len(UNITS) - 1
PLANE = (2, 2), (0, 1), (1, 0), (2, 1), (3, 2), (1, 2), (2, 3), (0, 3), (3, 0), (1, 1), (3, 3), (0, 2), (2, 0), (1, 3), (3, 1)
ORDER = (
    "y0 z0 z1 z2",
    "g0 g1 r0 a0",
    "p0 g2 p1 r1",
    "a1 s0 g3 p2",
    "s1 r2 a2 q0",
    "g4 f0 p3 g5",
    "s2 f1 q1 g6",
    "p4 f2 s3 p5",
    "g7 q2 p6 s4",
    "q3 s5 p7 s6",
    "q4 q5 s7 q6",
    "q7",
)


def halves(value):
    high = value.astype(BF16)
    return high, (value - high.astype(F32)).astype(BF16)


def kernel(x_ref, o_ref, X, Xh, Xl, Gp, R1, R2, S1, R3, R4, G, Gh, Gl, O, Oh, Ol, T, ss, rs):
    x, z, core = lax.axis_index("x"), lax.axis_index("z"), lax.axis_index("core")
    y = lax.axis_index("y_hi") * 2 + lax.axis_index("y_lo")
    v = jnp.where(core == 0, y, x)
    u = jnp.where(core == 0, x, y)

    def wrap(i):
        return lax.rem(i + 4, 4)

    def place(dv=0, du=0):
        vv, uu = wrap(v + dv), wrap(u + du)
        return jnp.where(core == 0, uu, vv), jnp.where(core == 0, vv, uu)

    def device(dv=0, du=0, dz=0, other=False):
        px, py = place(dv, du)
        return {
            "x": px,
            "y_hi": py // 2,
            "y_lo": lax.rem(py, 2),
            "z": wrap(z + dz),
            "core": 1 - core if other else core,
        }

    def columns(px, py):
        return pl.ds(pl.multiple_of((px * 4 + py) * WIDTH, WIDTH), WIDTH)

    count = [0]
    leaving = []

    def fresh(size):
        i = count[0]
        count[0] += 1
        leaving.append((i, size))
        return i

    def send(i, src, dst, **to):
        pltpu.make_async_remote_copy(
            src_ref=src, dst_ref=dst, send_sem=ss.at[i], recv_sem=rs.at[i], device_id=device(**to), device_id_type=MESH
        ).start()

    def send_one(src, dst, **to):
        i = fresh(src)
        send(i, src, dst, **to)
        return i, src

    def arrive(pair):
        i, size = pair
        pltpu.make_async_copy(size, size, rs.at[i]).wait()

    peers = [dict(dv=dv, du=du) for dv, du in PLANE] + [dict(dz=1), dict(dz=-1), dict(other=True)]
    barrier = pltpu.get_barrier_semaphore()
    for peer in peers:
        pl.semaphore_signal(barrier, inc=1, device_id=device(**peer), device_id_type=MESH)
    pl.semaphore_wait(barrier, len(peers))

    def band(dz=0, other=False):
        return wrap(z + dz) * 2 + (1 - core if other else core)

    mine, sibling = band(), band(0, True)
    near = [band(-1), band(1), band(-1, True), band(1, True)]
    away = [band(2), band(2, True)]
    rows = [[(mine, j) for j in range(GROUPS)], [(sibling, j) for j in range(GROUPS)]]
    rows += [[(b, j) for b in near] for j in range(GROUPS)]
    rows += [[(b, j) for b in away] for j in range(GROUPS)]

    i_out = fresh(x_ref.at[:, :, pl.ds(0, 15 * WIDTH)])
    i_in = [i_out, count[0], count[0] + 1, count[0] + 2]
    count[0] += 3

    def scatter(i, groups, dv, du):
        pltpu.make_async_remote_copy(
            src_ref=x_ref.at[groups, :, columns(*place(dv, du))],
            dst_ref=X.at[mine, groups, v, u],
            send_sem=ss.at[i_out],
            recv_sem=rs.at[i],
            device_id=device(dv=dv, du=du),
            device_id_type=MESH,
        ).start()

    for du in (1, 3, 2):
        scatter(i_in[3], pl.ds(0, GROUPS), 0, du)
    pltpu.make_async_copy(x_ref.at[:, :, columns(x, y)], X.at[mine, :, v, u], rs.at[i_in[3]]).start()
    for j in range(GROUPS):
        for dv, du in PLANE:
            if dv:
                scatter(i_in[j], j, dv, du)

    def dot_t(a, b):
        return lax.dot_general(a, b, (((1,), (1,)), ((), ())), preferred_element_type=F32)

    def dot(a, b):
        return jnp.dot(a, b, preferred_element_type=F32)

    def split(buf, high, low, c):
        for i, (b, j) in enumerate(rows[c]):
            at = slice((FIRST[c] + i) * LANES, (FIRST[c] + i + 1) * LANES)
            high[at, :], low[at, :] = halves(buf[b, j].reshape(LANES, WIDTH))

    vp, vm, v2 = wrap(v + 1), wrap(v - 1), wrap(v + 2)
    up, down, up2, down2, side = {}, {}, {}, {}, {}
    r1, r2, r3, r4 = {}, {}, {}, {}
    side["own"] = (fresh(X.at[0]), X.at[0])

    first = X.at[mine, :, v]
    i_first = [fresh(first), fresh(first)]

    def y_step(_):
        arrive((i_in[3], first))
        send(i_first[0], first, first, dz=1)
        send(i_first[1], first, first, dz=-1)
        send(side["own"][0], first, first, other=True)

    def z_step(j):
        size = X.at[0, j, pl.ds(0, 3)]
        arrive((i_in[j], size))
        up[j], down[j] = (fresh(size), size), (fresh(size), size)
        for to, i in ((dict(dz=1), up[j][0]), (dict(dz=-1), down[j][0]), (dict(other=True), side["own"][0])):
            for vv in (vp, v2, vm):
                part = X.at[mine, j, vv]
                send(i, part, part, **to)

    def r_step(j):
        if j == 0:
            arrive((i_first[0], first))
            arrive((i_first[1], first))
        arrive(up[j])
        half = X.at[near[0], j, pl.ds(0, 2)]
        up2[j] = send_one(half, half, dz=1)
        arrive(down[j])
        half = X.at[near[1], j, pl.ds(2, 2)]
        down2[j] = send_one(half, half, dz=-1)

    def a_step(j):
        side[j] = (fresh(X.at[0, pl.ds(0, 2)]), X.at[0, pl.ds(0, 2)])
        for b in near[:2]:
            send(side[j][0], X.at[b, j], X.at[b, j], other=True)

    def f_step(j):
        arrive(up2[j])
        arrive(down2[j])
        part = X.at[away[0], j]
        side[GROUPS + j] = send_one(part, part, other=True)

    def g_step(c):
        if c:
            arrive(side["own" if c == 1 else c - 2])
        split(X, Xh, Xl, c)
        at = CHUNK[c]
        ah, al, bh, bl = Xh[:BAND, :], Xl[:BAND, :], Xh[at, :], Xl[at, :]
        term = dot_t(ah, bh) + (dot_t(al, bh) + dot_t(ah, bl))
        Gp[:, :, :, :, at] = term.reshape(GROUPS, 4, 4, 8, LANES * UNITS[c])
        r1[c] = (
            send_one(Gp.at[:, v2, pl.ds(0, 2), :, at], R1.at[0, :, :, :, at], dv=1),
            send_one(Gp.at[:, v2, pl.ds(2, 2), :, at], R1.at[1, :, :, :, at], dv=-1),
        )

    def p_step(c):
        at = CHUNK[c]
        arrive(r1[c][0])
        Gp[:, vp, 0:2, :, at] += R1[0, :, :, :, at]
        first = send_one(Gp.at[:, vp, :, :, at], R2.at[0, :, :, :, at], dv=1)
        arrive(r1[c][1])
        Gp[:, vm, 2:4, :, at] += R1[1, :, :, :, at]
        r2[c] = (first, send_one(Gp.at[:, vm, :, :, at], R2.at[1, :, :, :, at], dv=-1))

    def s_step(c):
        at = CHUNK[c]
        for pair in r2[c]:
            arrive(pair)
        S1[:, :, :, at] = Gp[:, v, :, :, at] + (R2[0, :, :, :, at] + R2[1, :, :, :, at])
        if c == LAST:
            r3[c] = (fresh(R4), R4)
            for d in (1, 3, 2):
                send(r3[c][0], S1.at[:, :, :, at], R4.at[d - 1], du=d)
            return
        size = R3.at[:, :, :, at]
        r3[c] = (fresh(size), size)
        for d in (1, 3, 2):
            send(r3[c][0], S1.at[:, wrap(u + d), :, at], R3.at[d - 1, :, :, at], du=d)

    def q_step(c):
        at = CHUNK[c]
        arrive(r3[c])
        if c == LAST:
            G[:, v, :, :, at] = (S1[:, :, :, at] + R4[0]) + (R4[1] + R4[2])
            return
        G[:, v, u, :, at] = (S1[:, u, :, at] + R3[0, :, :, at]) + (R3[1, :, :, at] + R3[2, :, :, at])
        r4[c] = (fresh(r3[c][1]), r3[c][1])
        mine_of = G.at[:, v, u, :, at]
        for d in (1, 3, 2):
            send(r4[c][0], mine_of, mine_of, du=d)

    steps = dict(y=y_step, z=z_step, r=r_step, a=a_step, f=f_step, g=g_step, p=p_step, s=s_step, q=q_step)
    for line in ORDER:
        for step in line.split():
            steps[step[0]](int(step[1:]))
    for c in range(LAST):
        arrive(r4[c])

    def forward(vv, uu, dv):
        part = G.at[:, vv, uu]
        return send_one(part, part, dv=dv)

    rise = [forward(v, i, 1) for i in range(4)]
    fall = [forward(v, 3 - i, -1) for i in range(4)]
    rise2, fall2 = [], []

    takes = [((v, 0, 2), (v, 2, 2))]
    takes += [((vm, i, 1), (vp, 3 - i, 1)) for i in range(4)]
    takes += [((v2, i, 1), (v2, 3 - i, 1)) for i in range(2)]
    o_up, o_down, o_up2, o_down2 = [], [], [], []
    o_side = {key: (fresh(O.at[0]), O.at[0]) for key in ("own", "low", "high", "far")}

    def part_of(b, take):
        vv, first, n = take
        return O.at[b, :, vv, pl.ds(first, n)]

    def across(key, b, *parts):
        for take in parts:
            send(o_side[key][0], part_of(b, take), part_of(b, take), other=True)

    def once(k):
        at = []
        for vv, first, n in takes[k]:
            for j in range(GROUPS):
                h, l = halves(G[j, vv, pl.ds(first, n)].reshape(8 * n, ROWS))
                at.append((j, vv, first, n, h, l))
        high = jnp.concatenate([part[4] for part in at], axis=0)
        low = jnp.concatenate([part[5] for part in at], axis=0)
        m = high.shape[0]
        first_two = dot(jnp.concatenate([high, low], axis=0), Xh[...])
        result = first_two[:m] + (first_two[m:] + dot(high, Xl[...]))
        row = 0
        for j, vv, first, n, _, _ in at:
            O[mine, j, vv, pl.ds(first, n)] = result[row : row + 8 * n].reshape(n, 8, WIDTH)
            row += 8 * n
        a, b = takes[k]
        size = O.at[0, :, 0, pl.ds(0, 2 * a[2])]
        o_up.append((fresh(size), size))
        o_down.append((fresh(size), size))
        for take in (a, b):
            send(o_up[k][0], part_of(mine, take), part_of(mine, take), dz=1)
        for take in (b, a):
            send(o_down[k][0], part_of(mine, take), part_of(mine, take), dz=-1)
        across("own", mine, a, b)

    def pass_on(k):
        a, b = takes[k]
        arrive(o_up[k])
        o_up2.append(send_one(part_of(near[0], a), part_of(near[0], a), dz=1))
        arrive(o_down[k])
        o_down2.append(send_one(part_of(near[1], b), part_of(near[1], b), dz=-1))
        across("low", near[0], a, b)
        across("high", near[1], a, b)

    def far(k):
        arrive(o_up2[k])
        arrive(o_down2[k])
        across("far", away[0], *takes[k])

    once(0)
    for k in range(1, 7):
        if k < 5:
            arrive(rise[k - 1])
            if k < 3:
                rise2.append(forward(vm, k - 1, 1))
            arrive(fall[k - 1])
            if k < 3:
                fall2.append(forward(vp, 4 - k, -1))
        else:
            arrive(rise2[k - 5])
            arrive(fall2[k - 5])
        once(k)
        if k > 1:
            pass_on(k - 2)
        if k > 3:
            far(k - 4)
    for j in range(GROUPS):
        at = slice(j * LANES, (j + 1) * LANES)
        Gh[at, :], Gl[at, :] = halves(G[j].reshape(LANES, ROWS))

    def twice(c):
        split(O, Oh, Ol, c)
        at = CHUNK[c]
        gh, gl, oh, ol = Gh[:, at], Gl[:, at], Oh[at, :], Ol[at, :]
        term = (dot(gh, oh) + (dot(gl, oh) + dot(gh, ol))).reshape(GROUPS, 4, 4, 8, WIDTH)
        T[...] = T[...] + term if c else term

    twice(0)
    pass_on(5)
    far(3)
    arrive(o_side["own"])
    twice(1)
    pass_on(6)
    far(4)
    arrive(o_side["low"])
    arrive(o_side["high"])
    for c in (2, 3, 4):
        twice(c)
    far(5)
    far(6)
    arrive(o_side["far"])
    for c in (5, 6, 7):
        twice(c)
    T[...] = FACTOR * (3.4445 * X[mine] - 4.775 * O[mine] + 2.0315 * T[...])

    before = list(leaving)
    i_out = fresh(o_ref.at[:, :, pl.ds(0, 15 * WIDTH)])
    mine_at = o_ref.at[:, :, columns(x, y)]
    for dv, du in PLANE:
        send(i_out, T.at[:, wrap(v + dv), wrap(u + du)], mine_at, dv=dv, du=du)
    pltpu.make_async_copy(T.at[:, v, u], mine_at, rs.at[i_out]).start()
    for i, size in before:
        pltpu.make_async_copy(size, size, ss.at[i]).wait()
    arrive((i_out, o_ref))
    for i, size in leaving[len(before) :]:
        pltpu.make_async_copy(size, size, ss.at[i]).wait()
    if count[0] > N_SEMS:
        raise ValueError(count[0])


def per_device(iterate):
    vmem = pl.BlockSpec(memory_space=pltpu.VMEM)
    whole, gram, band = (BANDS, GROUPS, 4, 4, 8, WIDTH), (GROUPS, 4, 4, 8, ROWS), (BAND, ROWS)
    shapes = [
        (whole, F32),
        ((ROWS, WIDTH), BF16),
        ((ROWS, WIDTH), BF16),
        (gram, F32),
        ((2, GROUPS, 2, 8, ROWS), F32),
        ((2, GROUPS, 4, 8, ROWS), F32),
        ((GROUPS, 4, 8, ROWS), F32),
        ((3, GROUPS, 8, ROWS), F32),
        ((3, GROUPS, 4, 8, LANES * UNITS[-1]), F32),
        (gram, F32),
        (band, BF16),
        (band, BF16),
        (whole, F32),
        ((ROWS, WIDTH), BF16),
        ((ROWS, WIDTH), BF16),
        ((GROUPS, 4, 4, 8, WIDTH), F32),
    ]
    update = pl.pallas_call(
        kernel,
        out_shape=jax.ShapeDtypeStruct((GROUPS, 8, COLS), F32),
        in_specs=[vmem],
        out_specs=vmem,
        scratch_shapes=[pltpu.VMEM(shape, dtype) for shape, dtype in shapes]
        + [pltpu.SemaphoreType.DMA((N_SEMS,)), pltpu.SemaphoreType.DMA((N_SEMS,))],
        compiler_params=pltpu.CompilerParams(
            collective_id=0, has_side_effects=True, vmem_limit_bytes=50 * 1024 * 1024
        ),
        cost_estimate=pl.CostEstimate(
            flops=6 * 3 * BAND * ROWS * WIDTH, bytes_accessed=2 * 4 * GROUPS * 8 * COLS, transcendentals=0
        ),
    )(iterate.reshape(GROUPS, 8, COLS))
    return update.reshape(GROUPS * 8, COLS)


def solution(mesh):
    fine = Mesh(mesh.devices.reshape(2, 4, 2, 4, 2), AXES)
    spec = P(AXES, None)
    return jax.shard_map(per_device, mesh=fine, in_specs=(spec,), out_specs=spec, check_vma=False)
```

```python
import math

import jax
import jax.numpy as jnp
from jax import lax
from jax.experimental import pallas as pl
from jax.experimental.pallas import tpu as pltpu
from jax.sharding import Mesh, PartitionSpec as P

AXES = ("y_lo", "z", "core", "x", "y_hi")
BANDS = 8
GROUPS = 3
LANES = 128
BAND = GROUPS * LANES
ROWS = BANDS * BAND
WIDTH = 512
COLS = 16 * WIDTH
FACTOR = 0.2 * math.sqrt(max(ROWS, COLS))
F32, BF16 = jnp.float32, jnp.bfloat16
MESH = pl.DeviceIdType.MESH
N_SEMS = 117
UNITS = (3, 3, 4, 4, 4, 2, 2, 2)
FIRST = tuple(sum(UNITS[:c]) for c in range(len(UNITS)))
CHUNK = tuple(slice(LANES * a, LANES * (a + n)) for a, n in zip(FIRST, UNITS))
LAST = len(UNITS) - 1
PLANE = (2, 2), (0, 1), (1, 0), (2, 1), (3, 2), (1, 2), (2, 3), (0, 3), (3, 0), (1, 1), (3, 3), (0, 2), (2, 0), (1, 3), (3, 1)
ORDER = (
    "y0 z0 z1 z2",
    "g0 g1 r0 a0",
    "p0 g2 p1 r1",
    "a1 s0 g3 p2",
    "s1 r2 a2 q0",
    "g4 f0 p3 g5",
    "s2 f1 q1 g6",
    "p4 f2 s3 p5",
    "g7 q2 p6 s4",
    "q3 s5 p7 s6",
    "q4 q5 s7 q6",
    "q7",
)


def halves(value):
    high = value.astype(BF16)
    return high, (value - high.astype(F32)).astype(BF16)


def kernel(x_ref, o_ref, X, Xh, Xl, Gp, R1, R2, S1, R3, R4, G, Gh, Gl, O, Oh, Ol, T, ss, rs):
    x, z, core = lax.axis_index("x"), lax.axis_index("z"), lax.axis_index("core")
    y = lax.axis_index("y_hi") * 2 + lax.axis_index("y_lo")
    v = jnp.where(core == 0, y, x)
    u = jnp.where(core == 0, x, y)

    def wrap(i):
        return lax.rem(i + 4, 4)

    def place(dv=0, du=0):
        vv, uu = wrap(v + dv), wrap(u + du)
        return jnp.where(core == 0, uu, vv), jnp.where(core == 0, vv, uu)

    def device(dv=0, du=0, dz=0, other=False):
        px, py = place(dv, du)
        return {
            "x": px,
            "y_hi": py // 2,
            "y_lo": lax.rem(py, 2),
            "z": wrap(z + dz),
            "core": 1 - core if other else core,
        }

    def columns(px, py):
        return pl.ds(pl.multiple_of((px * 4 + py) * WIDTH, WIDTH), WIDTH)

    count = [0]
    leaving = []

    def fresh(size):
        i = count[0]
        count[0] += 1
        leaving.append((i, size))
        return i

    def send(i, src, dst, **to):
        pltpu.make_async_remote_copy(
            src_ref=src, dst_ref=dst, send_sem=ss.at[i], recv_sem=rs.at[i], device_id=device(**to), device_id_type=MESH
        ).start()

    def send_one(src, dst, **to):
        i = fresh(src)
        send(i, src, dst, **to)
        return i, src

    def arrive(pair):
        i, size = pair
        pltpu.make_async_copy(size, size, rs.at[i]).wait()

    peers = [dict(dv=dv, du=du) for dv, du in PLANE] + [dict(dz=1), dict(dz=-1), dict(other=True)]
    barrier = pltpu.get_barrier_semaphore()
    for peer in peers:
        pl.semaphore_signal(barrier, inc=1, device_id=device(**peer), device_id_type=MESH)
    pl.semaphore_wait(barrier, len(peers))

    def band(dz=0, other=False):
        return wrap(z + dz) * 2 + (1 - core if other else core)

    mine, sibling = band(), band(0, True)
    near = [band(-1), band(1), band(-1, True), band(1, True)]
    away = [band(2), band(2, True)]
    rows = [[(mine, j) for j in range(GROUPS)], [(sibling, j) for j in range(GROUPS)]]
    rows += [[(b, j) for b in near] for j in range(GROUPS)]
    rows += [[(b, j) for b in away] for j in range(GROUPS)]

    i_out = fresh(x_ref.at[:, :, pl.ds(0, 15 * WIDTH)])
    i_in = [i_out, count[0], count[0] + 1, count[0] + 2]
    count[0] += 3

    def scatter(i, groups, dv, du):
        pltpu.make_async_remote_copy(
            src_ref=x_ref.at[groups, :, columns(*place(dv, du))],
            dst_ref=X.at[mine, groups, v, u],
            send_sem=ss.at[i_out],
            recv_sem=rs.at[i],
            device_id=device(dv=dv, du=du),
            device_id_type=MESH,
        ).start()

    for du in (1, 3, 2):
        scatter(i_in[3], pl.ds(0, GROUPS), 0, du)
    pltpu.make_async_copy(x_ref.at[:, :, columns(x, y)], X.at[mine, :, v, u], rs.at[i_in[3]]).start()
    for j in range(GROUPS):
        for dv, du in PLANE:
            if dv:
                scatter(i_in[j], j, dv, du)

    def dot_t(a, b):
        return lax.dot_general(a, b, (((1,), (1,)), ((), ())), preferred_element_type=F32)

    def dot(a, b):
        return jnp.dot(a, b, preferred_element_type=F32)

    def split(buf, high, low, c):
        for i, (b, j) in enumerate(rows[c]):
            at = slice((FIRST[c] + i) * LANES, (FIRST[c] + i + 1) * LANES)
            high[at, :], low[at, :] = halves(buf[b, j].reshape(LANES, WIDTH))

    vp, vm, v2 = wrap(v + 1), wrap(v - 1), wrap(v + 2)
    up, down, up2, down2, side = {}, {}, {}, {}, {}
    r1, r2, r3, r4 = {}, {}, {}, {}
    side["own"] = (fresh(X.at[0]), X.at[0])

    first = X.at[mine, :, v]
    i_first = [fresh(first), fresh(first)]

    def y_step(_):
        arrive((i_in[3], first))
        send(i_first[0], first, first, dz=1)
        send(i_first[1], first, first, dz=-1)
        send(side["own"][0], first, first, other=True)

    def z_step(j):
        size = X.at[0, j, pl.ds(0, 3)]
        arrive((i_in[j], size))
        up[j], down[j] = (fresh(size), size), (fresh(size), size)
        for to, i in ((dict(dz=1), up[j][0]), (dict(dz=-1), down[j][0]), (dict(other=True), side["own"][0])):
            for vv in (vp, v2, vm):
                part = X.at[mine, j, vv]
                send(i, part, part, **to)

    def r_step(j):
        if j == 0:
            arrive((i_first[0], first))
            arrive((i_first[1], first))
        arrive(up[j])
        half = X.at[near[0], j, pl.ds(0, 2)]
        up2[j] = send_one(half, half, dz=1)
        arrive(down[j])
        half = X.at[near[1], j, pl.ds(2, 2)]
        down2[j] = send_one(half, half, dz=-1)

    def a_step(j):
        side[j] = (fresh(X.at[0, pl.ds(0, 2)]), X.at[0, pl.ds(0, 2)])
        for b in near[:2]:
            send(side[j][0], X.at[b, j], X.at[b, j], other=True)

    def f_step(j):
        arrive(up2[j])
        arrive(down2[j])
        part = X.at[away[0], j]
        side[GROUPS + j] = send_one(part, part, other=True)

    def g_step(c):
        if c:
            arrive(side["own" if c == 1 else c - 2])
        split(X, Xh, Xl, c)
        at = CHUNK[c]
        ah, al, bh, bl = Xh[:BAND, :], Xl[:BAND, :], Xh[at, :], Xl[at, :]
        term = dot_t(ah, bh) + (dot_t(al, bh) + dot_t(ah, bl))
        Gp[:, :, :, :, at] = term.reshape(GROUPS, 4, 4, 8, LANES * UNITS[c])
        r1[c] = (
            send_one(Gp.at[:, v2, pl.ds(0, 2), :, at], R1.at[0, :, :, :, at], dv=1),
            send_one(Gp.at[:, v2, pl.ds(2, 2), :, at], R1.at[1, :, :, :, at], dv=-1),
        )

    def p_step(c):
        at = CHUNK[c]
        arrive(r1[c][0])
        Gp[:, vp, 0:2, :, at] += R1[0, :, :, :, at]
        first = send_one(Gp.at[:, vp, :, :, at], R2.at[0, :, :, :, at], dv=1)
        arrive(r1[c][1])
        Gp[:, vm, 2:4, :, at] += R1[1, :, :, :, at]
        r2[c] = (first, send_one(Gp.at[:, vm, :, :, at], R2.at[1, :, :, :, at], dv=-1))

    def s_step(c):
        at = CHUNK[c]
        for pair in r2[c]:
            arrive(pair)
        S1[:, :, :, at] = Gp[:, v, :, :, at] + (R2[0, :, :, :, at] + R2[1, :, :, :, at])
        if c == LAST:
            r3[c] = (fresh(R4), R4)
            for d in (1, 3, 2):
                send(r3[c][0], S1.at[:, :, :, at], R4.at[d - 1], du=d)
            return
        size = R3.at[:, :, :, at]
        r3[c] = (fresh(size), size)
        for d in (1, 3, 2):
            send(r3[c][0], S1.at[:, wrap(u + d), :, at], R3.at[d - 1, :, :, at], du=d)

    def q_step(c):
        at = CHUNK[c]
        arrive(r3[c])
        if c == LAST:
            G[:, v, :, :, at] = (S1[:, :, :, at] + R4[0]) + (R4[1] + R4[2])
            return
        G[:, v, u, :, at] = (S1[:, u, :, at] + R3[0, :, :, at]) + (R3[1, :, :, at] + R3[2, :, :, at])
        r4[c] = (fresh(r3[c][1]), r3[c][1])
        mine_of = G.at[:, v, u, :, at]
        for d in (1, 3, 2):
            send(r4[c][0], mine_of, mine_of, du=d)

    steps = dict(y=y_step, z=z_step, r=r_step, a=a_step, f=f_step, g=g_step, p=p_step, s=s_step, q=q_step)
    for line in ORDER:
        for step in line.split():
            steps[step[0]](int(step[1:]))
    for c in range(LAST):
        arrive(r4[c])

    def forward(vv, uu, dv):
        part = G.at[:, vv, uu]
        return send_one(part, part, dv=dv)

    rise = [forward(v, i, 1) for i in range(4)]
    fall = [forward(v, 3 - i, -1) for i in range(4)]
    rise2, fall2 = [], []

    takes = [((v, 0, 2), (v, 2, 2))]
    takes += [((vm, i, 1), (vp, 3 - i, 1)) for i in range(4)]
    takes += [((v2, i, 1), (v2, 3 - i, 1)) for i in range(2)]
    o_up, o_down, o_up2, o_down2 = [], [], [], []
    o_side = {key: (fresh(O.at[0]), O.at[0]) for key in ("own", "low", "high", "far")}

    def part_of(b, take):
        vv, first, n = take
        return O.at[b, :, vv, pl.ds(first, n)]

    def across(key, b, *parts):
        for take in parts:
            send(o_side[key][0], part_of(b, take), part_of(b, take), other=True)

    def once(k):
        at = []
        for vv, first, n in takes[k]:
            for j in range(GROUPS):
                h, l = halves(G[j, vv, pl.ds(first, n)].reshape(8 * n, ROWS))
                at.append((j, vv, first, n, h, l))
        high = jnp.concatenate([part[4] for part in at], axis=0)
        low = jnp.concatenate([part[5] for part in at], axis=0)
        m = high.shape[0]
        first_two = dot(jnp.concatenate([high, low], axis=0), Xh[...])
        result = first_two[:m] + (first_two[m:] + dot(high, Xl[...]))
        row = 0
        for j, vv, first, n, _, _ in at:
            O[mine, j, vv, pl.ds(first, n)] = result[row : row + 8 * n].reshape(n, 8, WIDTH)
            row += 8 * n
        a, b = takes[k]
        size = O.at[0, :, 0, pl.ds(0, 2 * a[2])]
        o_up.append((fresh(size), size))
        o_down.append((fresh(size), size))
        for take in (a, b):
            send(o_up[k][0], part_of(mine, take), part_of(mine, take), dz=1)
        for take in (b, a):
            send(o_down[k][0], part_of(mine, take), part_of(mine, take), dz=-1)
        across("own", mine, a, b)

    def pass_on(k):
        a, b = takes[k]
        arrive(o_up[k])
        o_up2.append(send_one(part_of(near[0], a), part_of(near[0], a), dz=1))
        arrive(o_down[k])
        o_down2.append(send_one(part_of(near[1], b), part_of(near[1], b), dz=-1))
        across("low", near[0], a, b)
        across("high", near[1], a, b)

    def far(k):
        arrive(o_up2[k])
        arrive(o_down2[k])
        across("far", away[0], *takes[k])

    once(0)
    for k in range(1, 7):
        if k < 5:
            arrive(rise[k - 1])
            if k < 3:
                rise2.append(forward(vm, k - 1, 1))
            arrive(fall[k - 1])
            if k < 3:
                fall2.append(forward(vp, 4 - k, -1))
        else:
            arrive(rise2[k - 5])
            arrive(fall2[k - 5])
        once(k)
        if k == 1:
            pass_on(0)
        if k > 2:
            pass_on(k - 2)
        if k > 3:
            far(k - 4)
    for j in range(GROUPS):
        at = slice(j * LANES, (j + 1) * LANES)
        Gh[at, :], Gl[at, :] = halves(G[j].reshape(LANES, ROWS))

    def twice(c):
        split(O, Oh, Ol, c)
        at = CHUNK[c]
        gh, gl, oh, ol = Gh[:, at], Gl[:, at], Oh[at, :], Ol[at, :]
        term = (dot(gh, oh) + (dot(gl, oh) + dot(gh, ol))).reshape(GROUPS, 4, 4, 8, WIDTH)
        T[...] = T[...] + term if c else term

    twice(0)
    pass_on(5)
    far(3)
    arrive(o_side["own"])
    twice(1)
    pass_on(6)
    far(4)
    arrive(o_side["low"])
    arrive(o_side["high"])
    for c in (2, 3, 4):
        twice(c)
    far(5)
    far(6)
    arrive(o_side["far"])
    for c in (5, 6, 7):
        twice(c)
    T[...] = FACTOR * (2.0315 * T[...] - 4.775 * O[mine])

    before = list(leaving)
    i_out = fresh(o_ref.at[:, :, pl.ds(0, 15 * WIDTH)])
    mine_at = o_ref.at[:, :, columns(x, y)]
    for dv, du in PLANE:
        send(i_out, T.at[:, wrap(v + dv), wrap(u + du)], mine_at, dv=dv, du=du)
    pltpu.make_async_copy(T.at[:, v, u], mine_at, rs.at[i_out]).start()
    for i, size in before:
        pltpu.make_async_copy(size, size, ss.at[i]).wait()
    arrive((i_out, o_ref))
    for i, size in leaving[len(before) :]:
        pltpu.make_async_copy(size, size, ss.at[i]).wait()
    if count[0] > N_SEMS:
        raise ValueError(count[0])


def per_device(iterate):
    anywhere = pl.BlockSpec(memory_space=pl.ANY)
    whole, gram, band = (BANDS, GROUPS, 4, 4, 8, WIDTH), (GROUPS, 4, 4, 8, ROWS), (BAND, ROWS)
    shapes = [
        (whole, F32),
        ((ROWS, WIDTH), BF16),
        ((ROWS, WIDTH), BF16),
        (gram, F32),
        ((2, GROUPS, 2, 8, ROWS), F32),
        ((2, GROUPS, 4, 8, ROWS), F32),
        ((GROUPS, 4, 8, ROWS), F32),
        ((3, GROUPS, 8, ROWS), F32),
        ((3, GROUPS, 4, 8, LANES * UNITS[-1]), F32),
        (gram, F32),
        (band, BF16),
        (band, BF16),
        (whole, F32),
        ((ROWS, WIDTH), BF16),
        ((ROWS, WIDTH), BF16),
        ((GROUPS, 4, 4, 8, WIDTH), F32),
    ]
    applied = pl.pallas_call(
        kernel,
        out_shape=jax.ShapeDtypeStruct((GROUPS, 8, COLS), F32),
        in_specs=[anywhere],
        out_specs=anywhere,
        scratch_shapes=[pltpu.VMEM(shape, dtype) for shape, dtype in shapes]
        + [pltpu.SemaphoreType.DMA((N_SEMS,)), pltpu.SemaphoreType.DMA((N_SEMS,))],
        compiler_params=pltpu.CompilerParams(
            collective_id=0, has_side_effects=True, vmem_limit_bytes=50 * 1024 * 1024
        ),
        cost_estimate=pl.CostEstimate(
            flops=6 * 3 * BAND * ROWS * WIDTH, bytes_accessed=2 * 4 * GROUPS * 8 * COLS, transcendentals=0
        ),
    )(iterate.reshape(GROUPS, 8, COLS))
    return FACTOR * 3.4445 * iterate + applied.reshape(GROUPS * 8, COLS)


def solution(mesh):
    fine = Mesh(mesh.devices.reshape(2, 4, 2, 4, 2), AXES)
    spec = P(AXES, None)
    return jax.shard_map(per_device, mesh=fine, in_specs=(spec,), out_specs=spec, check_vma=False)
```

```python
import math

import jax
import jax.numpy as jnp
from jax import lax
from jax.experimental import pallas as pl
from jax.experimental.pallas import tpu as pltpu
from jax.sharding import Mesh, PartitionSpec as P

AXES = ("y_lo", "z", "core", "x", "y_hi")
BANDS = 8
GROUPS = 3
LANES = 128
BAND = GROUPS * LANES
ROWS = BANDS * BAND
WIDTH = 512
COLS = 16 * WIDTH
FACTOR = 0.2 * math.sqrt(max(ROWS, COLS))
F32, BF16 = jnp.float32, jnp.bfloat16
MESH = pl.DeviceIdType.MESH
N_SEMS = 117
UNITS = (3, 3, 4, 4, 4, 2, 2, 2)
FIRST = tuple(sum(UNITS[:c]) for c in range(len(UNITS)))
CHUNK = tuple(slice(LANES * a, LANES * (a + n)) for a, n in zip(FIRST, UNITS))
LAST = len(UNITS) - 1
PLANE = (2, 2), (0, 1), (1, 0), (2, 1), (3, 2), (1, 2), (2, 3), (0, 3), (3, 0), (1, 1), (3, 3), (0, 2), (2, 0), (1, 3), (3, 1)
ORDER = (
    "y0 z0 z1 z2",
    "g0 g1 r0 a0",
    "p0 g2 p1 r1",
    "a1 s0 g3 p2",
    "s1 r2 a2 q0",
    "g4 f0 p3 g5",
    "s2 f1 q1 g6",
    "p4 f2 s3 p5",
    "g7 q2 p6 s4",
    "q3 s5 p7 s6",
    "q4 q5 s7 q6",
    "q7",
)


def halves(value):
    high = value.astype(BF16)
    return high, (value - high.astype(F32)).astype(BF16)


def kernel(x_ref, o_ref, X, Xh, Xl, Gp, R1, R2, S1, R3, R4, G, Gh, Gl, O, Oh, Ol, T, ss, rs):
    x, z, core = lax.axis_index("x"), lax.axis_index("z"), lax.axis_index("core")
    y = lax.axis_index("y_hi") * 2 + lax.axis_index("y_lo")
    v = jnp.where(core == 0, y, x)
    u = jnp.where(core == 0, x, y)

    def wrap(i):
        return lax.rem(i + 4, 4)

    def place(dv=0, du=0):
        vv, uu = wrap(v + dv), wrap(u + du)
        return jnp.where(core == 0, uu, vv), jnp.where(core == 0, vv, uu)

    def device(dv=0, du=0, dz=0, other=False):
        px, py = place(dv, du)
        return {
            "x": px,
            "y_hi": py // 2,
            "y_lo": lax.rem(py, 2),
            "z": wrap(z + dz),
            "core": 1 - core if other else core,
        }

    def columns(px, py):
        return pl.ds(pl.multiple_of((px * 4 + py) * WIDTH, WIDTH), WIDTH)

    count = [0]
    leaving = []

    def fresh(size):
        i = count[0]
        count[0] += 1
        leaving.append((i, size))
        return i

    def send(i, src, dst, **to):
        pltpu.make_async_remote_copy(
            src_ref=src, dst_ref=dst, send_sem=ss.at[i], recv_sem=rs.at[i], device_id=device(**to), device_id_type=MESH
        ).start()

    def send_one(src, dst, **to):
        i = fresh(src)
        send(i, src, dst, **to)
        return i, src

    def arrive(pair):
        i, size = pair
        pltpu.make_async_copy(size, size, rs.at[i]).wait()

    peers = [dict(dv=dv, du=du) for dv, du in PLANE] + [dict(dz=1), dict(dz=-1), dict(other=True)]
    barrier = pltpu.get_barrier_semaphore()
    for peer in peers:
        pl.semaphore_signal(barrier, inc=1, device_id=device(**peer), device_id_type=MESH)
    pl.semaphore_wait(barrier, len(peers))

    def band(dz=0, other=False):
        return wrap(z + dz) * 2 + (1 - core if other else core)

    mine, sibling = band(), band(0, True)
    near = [band(-1), band(1), band(-1, True), band(1, True)]
    away = [band(2), band(2, True)]
    rows = [[(mine, j) for j in range(GROUPS)], [(sibling, j) for j in range(GROUPS)]]
    rows += [[(b, j) for b in near] for j in range(GROUPS)]
    rows += [[(b, j) for b in away] for j in range(GROUPS)]

    i_out = fresh(x_ref.at[:, :, pl.ds(0, 15 * WIDTH)])
    i_in = [i_out, count[0], count[0] + 1, count[0] + 2]
    count[0] += 3

    def scatter(i, groups, dv, du):
        pltpu.make_async_remote_copy(
            src_ref=x_ref.at[groups, :, columns(*place(dv, du))],
            dst_ref=X.at[mine, groups, v, u],
            send_sem=ss.at[i_out],
            recv_sem=rs.at[i],
            device_id=device(dv=dv, du=du),
            device_id_type=MESH,
        ).start()

    for du in (1, 3, 2):
        scatter(i_in[3], pl.ds(0, GROUPS), 0, du)
    pltpu.make_async_copy(x_ref.at[:, :, columns(x, y)], X.at[mine, :, v, u], rs.at[i_in[3]]).start()
    for j in range(GROUPS):
        for dv, du in PLANE:
            if dv:
                scatter(i_in[j], j, dv, du)

    def dot_t(a, b):
        return lax.dot_general(a, b, (((1,), (1,)), ((), ())), preferred_element_type=F32)

    def dot(a, b):
        return jnp.dot(a, b, preferred_element_type=F32)

    def split(buf, high, low, c):
        for i, (b, j) in enumerate(rows[c]):
            at = slice((FIRST[c] + i) * LANES, (FIRST[c] + i + 1) * LANES)
            high[at, :], low[at, :] = halves(buf[b, j].reshape(LANES, WIDTH))

    vp, vm, v2 = wrap(v + 1), wrap(v - 1), wrap(v + 2)
    up, down, up2, down2, side = {}, {}, {}, {}, {}
    r1, r2, r3, r4 = {}, {}, {}, {}
    side["own"] = (fresh(X.at[0]), X.at[0])

    first = X.at[mine, :, v]
    i_first = [fresh(first), fresh(first)]

    def y_step(_):
        arrive((i_in[3], first))
        send(i_first[0], first, first, dz=1)
        send(i_first[1], first, first, dz=-1)
        send(side["own"][0], first, first, other=True)

    def z_step(j):
        size = X.at[0, j, pl.ds(0, 3)]
        arrive((i_in[j], size))
        up[j], down[j] = (fresh(size), size), (fresh(size), size)
        for to, i in ((dict(dz=1), up[j][0]), (dict(dz=-1), down[j][0]), (dict(other=True), side["own"][0])):
            for vv in (vp, v2, vm):
                part = X.at[mine, j, vv]
                send(i, part, part, **to)

    def r_step(j):
        if j == 0:
            arrive((i_first[0], first))
            arrive((i_first[1], first))
        arrive(up[j])
        half = X.at[near[0], j, pl.ds(0, 2)]
        up2[j] = send_one(half, half, dz=1)
        arrive(down[j])
        half = X.at[near[1], j, pl.ds(2, 2)]
        down2[j] = send_one(half, half, dz=-1)

    def a_step(j):
        side[j] = (fresh(X.at[0, pl.ds(0, 2)]), X.at[0, pl.ds(0, 2)])
        for b in near[:2]:
            send(side[j][0], X.at[b, j], X.at[b, j], other=True)

    def f_step(j):
        arrive(up2[j])
        arrive(down2[j])
        part = X.at[away[0], j]
        side[GROUPS + j] = send_one(part, part, other=True)

    def g_step(c):
        if c:
            arrive(side["own" if c == 1 else c - 2])
        split(X, Xh, Xl, c)
        at = CHUNK[c]
        ah, al, bh, bl = Xh[:BAND, :], Xl[:BAND, :], Xh[at, :], Xl[at, :]
        term = dot_t(ah, bh) + (dot_t(al, bh) + dot_t(ah, bl))
        Gp[:, :, :, :, at] = term.reshape(GROUPS, 4, 4, 8, LANES * UNITS[c])
        r1[c] = (
            send_one(Gp.at[:, v2, pl.ds(0, 2), :, at], R1.at[0, :, :, :, at], dv=1),
            send_one(Gp.at[:, v2, pl.ds(2, 2), :, at], R1.at[1, :, :, :, at], dv=-1),
        )

    def p_step(c):
        at = CHUNK[c]
        arrive(r1[c][0])
        Gp[:, vp, 0:2, :, at] += R1[0, :, :, :, at]
        first = send_one(Gp.at[:, vp, :, :, at], R2.at[0, :, :, :, at], dv=1)
        arrive(r1[c][1])
        Gp[:, vm, 2:4, :, at] += R1[1, :, :, :, at]
        r2[c] = (first, send_one(Gp.at[:, vm, :, :, at], R2.at[1, :, :, :, at], dv=-1))

    def s_step(c):
        at = CHUNK[c]
        for pair in r2[c]:
            arrive(pair)
        S1[:, :, :, at] = Gp[:, v, :, :, at] + (R2[0, :, :, :, at] + R2[1, :, :, :, at])
        if c == LAST:
            r3[c] = (fresh(R4), R4)
            for d in (1, 3, 2):
                send(r3[c][0], S1.at[:, :, :, at], R4.at[d - 1], du=d)
            return
        size = R3.at[:, :, :, at]
        r3[c] = (fresh(size), size)
        for d in (1, 3, 2):
            send(r3[c][0], S1.at[:, wrap(u + d), :, at], R3.at[d - 1, :, :, at], du=d)

    def q_step(c):
        at = CHUNK[c]
        arrive(r3[c])
        if c == LAST:
            G[:, v, :, :, at] = (S1[:, :, :, at] + R4[0]) + (R4[1] + R4[2])
            return
        G[:, v, u, :, at] = (S1[:, u, :, at] + R3[0, :, :, at]) + (R3[1, :, :, at] + R3[2, :, :, at])
        r4[c] = (fresh(r3[c][1]), r3[c][1])
        mine_of = G.at[:, v, u, :, at]
        for d in (1, 3, 2):
            send(r4[c][0], mine_of, mine_of, du=d)

    steps = dict(y=y_step, z=z_step, r=r_step, a=a_step, f=f_step, g=g_step, p=p_step, s=s_step, q=q_step)
    for line in ORDER:
        for step in line.split():
            steps[step[0]](int(step[1:]))
    for c in range(LAST):
        arrive(r4[c])

    def forward(vv, uu, dv):
        part = G.at[:, vv, uu]
        return send_one(part, part, dv=dv)

    rise = [forward(v, i, 1) for i in range(4)]
    fall = [forward(v, 3 - i, -1) for i in range(4)]
    rise2, fall2 = [], []

    takes = [((v, 0, 2), (v, 2, 2))]
    takes += [((vm, i, 1), (vp, 3 - i, 1)) for i in range(4)]
    takes += [((v2, i, 1), (v2, 3 - i, 1)) for i in range(2)]
    o_up, o_down, o_up2, o_down2 = [], [], [], []
    o_side = {key: (fresh(O.at[0]), O.at[0]) for key in ("own", "low", "high", "far")}

    def part_of(b, take):
        vv, first, n = take
        return O.at[b, :, vv, pl.ds(first, n)]

    def across(key, b, *parts):
        for take in parts:
            send(o_side[key][0], part_of(b, take), part_of(b, take), other=True)

    def once(k):
        at = []
        for vv, first, n in takes[k]:
            for j in range(GROUPS):
                h, l = halves(G[j, vv, pl.ds(first, n)].reshape(8 * n, ROWS))
                at.append((j, vv, first, n, h, l))
        high = jnp.concatenate([part[4] for part in at], axis=0)
        low = jnp.concatenate([part[5] for part in at], axis=0)
        m = high.shape[0]
        first_two = dot(jnp.concatenate([high, low], axis=0), Xh[...])
        result = first_two[:m] + (first_two[m:] + dot(high, Xl[...]))
        row = 0
        for j, vv, first, n, _, _ in at:
            O[mine, j, vv, pl.ds(first, n)] = result[row : row + 8 * n].reshape(n, 8, WIDTH)
            row += 8 * n
        a, b = takes[k]
        size = O.at[0, :, 0, pl.ds(0, 2 * a[2])]
        o_up.append((fresh(size), size))
        o_down.append((fresh(size), size))
        for take in (a, b):
            send(o_up[k][0], part_of(mine, take), part_of(mine, take), dz=1)
        for take in (b, a):
            send(o_down[k][0], part_of(mine, take), part_of(mine, take), dz=-1)
        across("own", mine, a, b)

    def pass_on(k):
        a, b = takes[k]
        arrive(o_up[k])
        o_up2.append(send_one(part_of(near[0], a), part_of(near[0], a), dz=1))
        arrive(o_down[k])
        o_down2.append(send_one(part_of(near[1], b), part_of(near[1], b), dz=-1))
        across("low", near[0], a, b)
        across("high", near[1], a, b)

    def far(k):
        arrive(o_up2[k])
        arrive(o_down2[k])
        across("far", away[0], *takes[k])

    once(0)
    for k in range(1, 7):
        if k < 5:
            arrive(rise[k - 1])
            if k < 3:
                rise2.append(forward(vm, k - 1, 1))
            arrive(fall[k - 1])
            if k < 3:
                fall2.append(forward(vp, 4 - k, -1))
        else:
            arrive(rise2[k - 5])
            arrive(fall2[k - 5])
        once(k)
        if k == 1:
            pass_on(0)
        if k > 2:
            pass_on(k - 2)
        if k > 3:
            far(k - 4)
    for j in range(GROUPS):
        at = slice(j * LANES, (j + 1) * LANES)
        Gh[at, :], Gl[at, :] = halves(G[j].reshape(LANES, ROWS))

    def term(*chunk):
        for c in chunk:
            split(O, Oh, Ol, c)
        at = slice(CHUNK[chunk[0]].start, CHUNK[chunk[-1]].stop)
        gh, gl, oh, ol = Gh[:, at], Gl[:, at], Oh[at, :], Ol[at, :]
        return (dot(gh, oh) + (dot(gl, oh) + dot(gh, ol))).reshape(GROUPS, 4, 4, 8, WIDTH)

    def twice(c):
        T[...] = T[...] + term(c) if c else term(c)

    twice(0)
    pass_on(5)
    far(3)
    arrive(o_side["own"])
    twice(1)
    pass_on(6)
    far(4)
    arrive(o_side["low"])
    arrive(o_side["high"])
    for c in (2, 3, 4):
        twice(c)
    far(5)
    far(6)
    arrive(o_side["far"])
    T[...] = FACTOR * (2.0315 * (T[...] + term(5, 6, 7)) - 4.775 * O[mine])

    before = list(leaving)
    i_out = fresh(o_ref.at[:, :, pl.ds(0, 15 * WIDTH)])
    mine_at = o_ref.at[:, :, columns(x, y)]
    for dv, du in PLANE:
        send(i_out, T.at[:, wrap(v + dv), wrap(u + du)], mine_at, dv=dv, du=du)
    pltpu.make_async_copy(T.at[:, v, u], mine_at, rs.at[i_out]).start()
    for i, size in before:
        pltpu.make_async_copy(size, size, ss.at[i]).wait()
    arrive((i_out, o_ref))
    for i, size in leaving[len(before) :]:
        pltpu.make_async_copy(size, size, ss.at[i]).wait()
    if count[0] > N_SEMS:
        raise ValueError(count[0])


def per_device(iterate):
    anywhere = pl.BlockSpec(memory_space=pl.ANY)
    whole, gram, band = (BANDS, GROUPS, 4, 4, 8, WIDTH), (GROUPS, 4, 4, 8, ROWS), (BAND, ROWS)
    shapes = [
        (whole, F32),
        ((ROWS, WIDTH), BF16),
        ((ROWS, WIDTH), BF16),
        (gram, F32),
        ((2, GROUPS, 2, 8, ROWS), F32),
        ((2, GROUPS, 4, 8, ROWS), F32),
        ((GROUPS, 4, 8, ROWS), F32),
        ((3, GROUPS, 8, ROWS), F32),
        ((3, GROUPS, 4, 8, LANES * UNITS[-1]), F32),
        (gram, F32),
        (band, BF16),
        (band, BF16),
        (whole, F32),
        ((ROWS, WIDTH), BF16),
        ((ROWS, WIDTH), BF16),
        ((GROUPS, 4, 4, 8, WIDTH), F32),
    ]
    applied = pl.pallas_call(
        kernel,
        out_shape=jax.ShapeDtypeStruct((GROUPS, 8, COLS), F32),
        in_specs=[anywhere],
        out_specs=anywhere,
        scratch_shapes=[pltpu.VMEM(shape, dtype) for shape, dtype in shapes]
        + [pltpu.SemaphoreType.DMA((N_SEMS,)), pltpu.SemaphoreType.DMA((N_SEMS,))],
        compiler_params=pltpu.CompilerParams(
            collective_id=0, has_side_effects=True, vmem_limit_bytes=50 * 1024 * 1024
        ),
        cost_estimate=pl.CostEstimate(
            flops=6 * 3 * BAND * ROWS * WIDTH, bytes_accessed=2 * 4 * GROUPS * 8 * COLS, transcendentals=0
        ),
    )(iterate.reshape(GROUPS, 8, COLS))
    return FACTOR * 3.4445 * iterate + applied.reshape(GROUPS * 8, COLS)


def solution(mesh):
    fine = Mesh(mesh.devices.reshape(2, 4, 2, 4, 2), AXES)
    spec = P(AXES, None)
    return jax.shard_map(per_device, mesh=fine, in_specs=(spec,), out_specs=spec, check_vma=False)
```
